32 devices in a mesh: dp: 2 (over core), expert: 4 (over y, x), tensor: 4 (over z).
Axes of the slice: x: 2, y: 2, z: 4, core: 2. Of those that a mesh axis runs over, the one named last changes fastest.
Arguments:
- tokens: bfloat16 [1024, 3072], P(('dp', 'expert')), may hold values from -6 to 6
- cotangent: bfloat16 [1024, 3072], P(('dp', 'expert')), may hold values from -6 to 6
- gate_weights: bfloat16 [1024, 2], P(('dp', 'expert')), may hold values from 0.099609375 to 0.8984375
- expert_ids: int32 [1024, 2], P(('dp', 'expert')), may hold values from 0 to 3, all different within a row; in each aligned block of 128 rows (0 to 127, 128 to 255, ...) at most 96 rows name the same one
- w_gate: bfloat16 [4, 3072, 8192], P('expert', 'dp', 'tensor'), may hold values from -0.109375 to 0.109375
- w_up: bfloat16 [4, 3072, 8192], P('expert', 'dp', 'tensor'), may hold values from -0.109375 to 0.109375
- w_down: bfloat16 [4, 3072, 8192], P('expert', 'dp', 'tensor'), may hold values from -0.0625 to 0.0625
Outputs:
- input_grad: bfloat16 [1024, 3072], P(('dp', 'expert'))
- gate_grad: bfloat16 [1024, 2], P(('dp', 'expert'))
- grad_gate: bfloat16 [4, 3072, 8192], P('expert', 'dp', 'tensor')
- grad_up: bfloat16 [4, 3072, 8192], P('expert', 'dp', 'tensor')
- grad_down: bfloat16 [4, 3072, 8192], P('expert', 'dp', 'tensor')
The draws below stay inside these ranges and needn't reach their ends.
Inputs may be any that keep to these rules, and one draw needn't show every extreme that they name: `expert_ids`: each token names 2 different experts. Among the 128 tokens of one block, no expert is named more than 96 times, and in some blocks one expert is named exactly 96 times.
All inputs are finite; a program needn't handle non-finite values.
Results may differ from the reference program's by a relative error of at most 0.025.
Values may be sent and summed in bfloat16 or wider, within the bound.
A program may use at most 128 MiB of HBM per device.

```python
import math
import jax
import jax.numpy as jnp
import numpy as np
from jax import lax

D = 3072
FF = 8192
TOP = 2
TOK_DEV = 128
EXPERTS = 4
CAP = 96
TOKENS = 1024
N_DP = 2
N_EXPERT = 4
N_TENSOR = 4


def block_scale(rng, dims, shards, low, high):
    gain, own = 1.0, jax.random.fold_in(rng, 6)
    for dim, shards_of in shards:
        steps = jnp.exp(jax.random.uniform(jax.random.fold_in(own, dim), (shards_of,), jnp.float32, low / len(shards), high / len(shards)))
        gain = gain * jnp.repeat(steps, dims[dim] // shards_of).reshape([-1 if axis == dim else 1 for axis in range(len(dims))])
    return gain


def deal_out(rng, own, number, rows, number_of, top, limit, skew):
    ranking = jax.random.permutation(rng, number_of)
    packed, common = load_shares(number_of, rows * top, limit, skew, True), load_shares(number_of, rows * top, limit, skew, False)
    places = jnp.arange(number_of)

    def named(tallies, offset_by):
        used = int((tallies > 0).sum())
        fixed = max(1, used // 4)
        shifted = fixed + (places - fixed + offset_by * (used - fixed)) % max(1, number_of - fixed)
        return jnp.zeros((number_of,), jnp.int32).at[ranking[jnp.where(places < fixed, places, shifted)]].set(jnp.asarray(tallies, jnp.int32))

    tallies = jnp.where(number % 4 == 0, named(packed, number // 4), named(common, number - number // 4 - 1))
    mixed = jax.random.permutation(jax.random.fold_in(own, 3), number_of)
    source_of, sink = mixed[0:number_of // 2 * 2:2], mixed[1:number_of // 2 * 2:2]
    margin = jnp.minimum(tallies[source_of] - 1, limit - tallies[sink]) // 2
    margin = jnp.where((source_of == ranking[0]) | (sink == ranking[0]) | (tallies[sink] == 0), 0, jnp.maximum(margin, 0))
    shifted = jax.random.randint(jax.random.fold_in(own, 4), (number_of // 2,), 0, 1 << 20) % (margin + 1)
    tallies = tallies.at[source_of].add(-shifted).at[sink].add(shifted)
    items = jnp.searchsorted(jnp.cumsum(tallies), jnp.arange(rows * top), side="right").astype(jnp.int32)
    listing = items.reshape(top, rows).T
    listing = listing[jax.random.permutation(jax.random.fold_in(own, 1), rows)]
    offset_by = jax.random.randint(jax.random.fold_in(own, 2), (rows, 1), 0, top)
    return jnp.take_along_axis(listing, (jnp.arange(top)[None, :] + offset_by) % top, axis=1)


def load_shares(count, total, limit, slope, full):
    loads = [(1 << 20) // math.isqrt(grade ** slope) + 1 for grade in range(1, count + 1)]
    largest = limit if full else min(limit, max(-(-total // count), total * loads[0] // sum(loads)))
    least = 1 if total - largest >= count - 1 else 0
    holding, spare = [largest] + [least] * (count - 1), total - largest - least * (count - 1)
    while spare > 0:
        candidates = [i for i in range(1, count) if holding[i] < largest] or [i for i in range(1, count) if holding[i] < limit]
        mass, left = sum([loads[i] for i in candidates]), spare
        for i in candidates:
            more = min(limit - holding[i], max(1, left * loads[i] // mass), spare)
            holding[i] = holding[i] + more
            spare = spare - more
    return np.array(holding)


def gaussian(own_key, extent, scale, bound, cuts=(), kind=jnp.bfloat16):
    result = scale * jax.random.normal(own_key, extent, jnp.float32)
    if cuts:
        result = result * block_scale(own_key, extent, cuts, -0.22, 0.18)
    return jnp.clip(result, -bound, bound).astype(kind)


def setup_inputs(seed: int = 0) -> dict:
    streams_of = jax.random.split(jax.random.key(seed), 8)
    tokens = gaussian(streams_of[0], (TOKENS, D), 1.0, 6.0, ((0, 8),))
    cotangent = gaussian(streams_of[1], (TOKENS, D), 1.0, 6.0, ((0, 8),))
    gate_weights = jnp.clip(0.099609375 + 0.7988281 * jax.random.uniform(streams_of[2], (TOKENS, TOP), jnp.float32) ** block_scale(streams_of[2], (TOKENS, TOP), ((0, 8),), -0.2, 0.2), 0.099609375, 0.8984375).astype(jnp.bfloat16)
    expert_ids_keys = jax.random.split(jax.random.fold_in(streams_of[3], 1), TOKENS // TOK_DEV)
    expert_ids_turns = jax.random.permutation(jax.random.fold_in(streams_of[3], 3), TOKENS // TOK_DEV)
    expert_ids = jax.vmap(lambda own, number: deal_out(jax.random.fold_in(streams_of[3], 2), own, number, TOK_DEV, EXPERTS, TOP, CAP, 2))(expert_ids_keys, expert_ids_turns).reshape((TOKENS, TOP))
    w_gate = gaussian(streams_of[4], (EXPERTS, D, FF), D ** -0.5, 0.109375, ((0, 4), (1, 2), (2, 4)))
    w_up = gaussian(streams_of[5], (EXPERTS, D, FF), D ** -0.5, 0.109375, ((0, 4), (1, 2), (2, 4)))
    w_down = gaussian(streams_of[6], (EXPERTS, D, FF), FF ** -0.5, 0.0625, ((0, 4), (1, 2), (2, 4)))
    return dict(tokens=tokens, cotangent=cotangent, gate_weights=gate_weights, expert_ids=expert_ids, w_gate=w_gate, w_up=w_up, w_down=w_down)


def slot_numbers(expert_ids, experts):
    labels = lax.broadcasted_iota(jnp.int32, (1, 1, experts), 2)
    onehot = (expert_ids[:, :, None] == labels).astype(jnp.int32).reshape(-1, experts)
    earlier = jnp.cumsum(onehot, axis=0) - onehot
    return jnp.sum(earlier * onehot, axis=1).astype(jnp.int32)


def entry_table(expert_ids, experts, capacity):
    flat_slot = slot_numbers(expert_ids, experts)
    target = expert_ids.reshape(-1).astype(jnp.int32) * capacity + flat_slot
    entry_count = expert_ids.shape[0] * expert_ids.shape[1]
    entries = jnp.full((experts * capacity,), entry_count, jnp.int32)
    entries = entries.at[target].set(jnp.arange(entry_count, dtype=jnp.int32))
    return target, entries


def fill_buffers(tokens, cotangent, gate_weights, entries):
    model_width = tokens.shape[1]
    zero_row = jnp.zeros((1, model_width), tokens.dtype)
    token_rows = (entries // 2).astype(jnp.int32)
    token_pad = jnp.concatenate([tokens, zero_row], 0)
    grad_pad = jnp.concatenate([cotangent, zero_row], 0)
    weight_pad = jnp.concatenate([gate_weights.reshape(-1), jnp.zeros((2,), gate_weights.dtype)], 0)
    return token_pad[token_rows], grad_pad[token_rows], weight_pad[entries]


def split_units(array):
    width = array.shape[1] // N_TENSOR
    return jnp.moveaxis(array.reshape(array.shape[0], N_TENSOR, width), 1, 0)


def reference(tokens, cotangent, gate_weights, expert_ids, w_gate, w_up, w_down):
    blocks = N_DP * N_EXPERT
    x_blocks = tokens.reshape(blocks, TOK_DEV, D)
    dy_blocks = cotangent.reshape(blocks, TOK_DEV, D)
    g_blocks = gate_weights.reshape(blocks, TOK_DEV, TOP)
    id_blocks = expert_ids.reshape(blocks, TOK_DEV, TOP)

    def table_of(block_ids):
        return entry_table(block_ids, EXPERTS, CAP)

    targets, entries = jax.vmap(table_of)(id_blocks)
    x_buf, dy_buf, g_buf = jax.vmap(fill_buffers)(x_blocks, dy_blocks, g_blocks, entries)

    def by_expert(buffer, columns):
        shaped = buffer.reshape((blocks, EXPERTS, CAP) + columns)
        moved = jnp.moveaxis(shaped, 1, 0)
        return moved.reshape((EXPERTS, blocks * CAP) + columns)

    x_rows = by_expert(x_buf, (D,))
    dy_rows = by_expert(dy_buf, (D,))
    g_rows = by_expert(g_buf, ())
    half_rows = N_EXPERT * CAP
    inner = (((1,), (1,)), ((), ()))
    outer = (((0,), (0,)), ((), ()))

    def dp_total(left, right):
        total = jnp.zeros((left.shape[1], right.shape[1]), jnp.float32)
        for member in range(N_DP):
            piece = lax.dot_general(left[member * half_rows:(member + 1) * half_rows],
                                    right[member * half_rows:(member + 1) * half_rows],
                                    outer, preferred_element_type=jnp.float32).astype(jnp.bfloat16)
            piece = lax.optimization_barrier(piece)
            total = total + piece.astype(jnp.float32)
        return total.astype(jnp.bfloat16)

    def per_expert(operands):
        rows_x, rows_dy, rows_gate, gate_full, up_full, down_full = operands
        gate_pre = jnp.dot(rows_x, gate_full, preferred_element_type=jnp.float32)
        up_pre = jnp.dot(rows_x, up_full, preferred_element_type=jnp.float32)
        sigma = jax.nn.sigmoid(gate_pre)
        active = gate_pre * sigma
        hidden = (active * up_pre).astype(jnp.bfloat16)
        back = jnp.dot(rows_dy, down_full, preferred_element_type=jnp.float32)
        factor = rows_gate.astype(jnp.float32)[:, None]
        hidden_grad = factor * back
        d_pre_gate = (hidden_grad * up_pre * sigma * (1.0 + gate_pre * (1.0 - sigma))).astype(jnp.bfloat16)
        d_pre_up = (hidden_grad * active).astype(jnp.bfloat16)
        scaled = (factor * rows_dy.astype(jnp.float32)).astype(jnp.bfloat16)

        def add_sliver(carry, pieces):
            input_total, gate_total = carry
            piece_gate, piece_up, piece_hidden, piece_back, weight_gate, weight_up = pieces
            part_input = (lax.dot_general(piece_gate, weight_gate, inner, preferred_element_type=jnp.float32)
                          + lax.dot_general(piece_up, weight_up, inner, preferred_element_type=jnp.float32)).astype(jnp.bfloat16)
            part_gate = jnp.sum(piece_hidden.astype(jnp.float32) * piece_back, axis=1).astype(jnp.bfloat16)
            part_input = lax.optimization_barrier(part_input)
            part_gate = lax.optimization_barrier(part_gate)
            return (input_total + part_input.astype(jnp.float32), gate_total + part_gate.astype(jnp.float32)), None

        row_count = rows_x.shape[0]
        start = (jnp.zeros((row_count, D), jnp.float32), jnp.zeros((row_count,), jnp.float32))
        (input_sum, gate_sum), _ = lax.scan(add_sliver, start,
                                            (split_units(d_pre_gate), split_units(d_pre_up), split_units(hidden),
                                             split_units(back), split_units(gate_full), split_units(up_full)))
        slot_input = input_sum.astype(jnp.bfloat16)
        slot_gate = gate_sum.astype(jnp.bfloat16)
        return (slot_input, slot_gate, dp_total(rows_x, d_pre_gate), dp_total(rows_x, d_pre_up),
                dp_total(scaled, hidden))

    slot_input, slot_gate, grad_gate, grad_up, grad_down = lax.map(
        per_expert, (x_rows, dy_rows, g_rows, w_gate, w_up, w_down))
    slot_input = jnp.moveaxis(slot_input.reshape(EXPERTS, blocks, CAP, D), 1, 0).reshape(blocks, EXPERTS * CAP, D)
    slot_gate = jnp.moveaxis(slot_gate.reshape(EXPERTS, blocks, CAP), 1, 0).reshape(blocks, EXPERTS * CAP)

    def combine(block_input, block_gate, target):
        rows = block_input[target].reshape(TOK_DEV, TOP, D)
        summed = jnp.sum(rows.astype(jnp.float32), axis=1).astype(jnp.bfloat16)
        return summed, block_gate[target].reshape(TOK_DEV, TOP)

    input_grad, gate_grad = jax.vmap(combine)(slot_input, slot_gate, targets)
    return (input_grad.reshape(TOKENS, D), gate_grad.reshape(TOKENS, TOP), grad_gate, grad_up, grad_down)
```

```python
import jax
import jax.numpy as jnp
from jax import lax
from jax.sharding import PartitionSpec as P

F32, BF16 = jnp.float32, jnp.bfloat16
PARTS = 2
BLOCKS = ("dp", "expert")


def dot(left, right, left_dim, right_dim):
    return lax.dot_general(
        left, right, (((left_dim,), (right_dim,)), ((), ())), preferred_element_type=F32
    )


def dp_sum(partial):
    count = lax.axis_size("dp")
    sent = partial.astype(BF16)
    total = partial
    for shift in range(1, count):
        moved = lax.ppermute(sent, "dp", [(i, (i + shift) % count) for i in range(count)])
        total = total + moved.astype(F32)
    return total


def on_device(tokens, cotangent, gate_weights, expert_ids, w_gate, w_up, w_down):
    experts = lax.axis_size("expert")
    count_dp = lax.axis_size("dp")
    count_tensor = lax.axis_size("tensor")
    blocks = count_dp * experts
    tok_count, model_width = tokens.shape
    capacity = tok_count * 3 // experts
    part = capacity // PARTS
    w_gate, w_up, w_down = w_gate[0], w_up[0], w_down[0]
    width, units = w_gate.shape
    rows = blocks * part

    labels = lax.broadcasted_iota(jnp.int32, (experts, 1, 1), 0)
    named = expert_ids[None] == labels
    mask = jnp.any(named, axis=2)
    weight = jnp.sum(jnp.where(named, gate_weights[None].astype(F32), 0.0), axis=2)
    earlier_row = lax.broadcasted_iota(jnp.int32, (tok_count, tok_count), 0)
    earlier_col = lax.broadcasted_iota(jnp.int32, (tok_count, tok_count), 1)
    before = (earlier_row < earlier_col).astype(BF16)
    slots = dot(mask.astype(BF16), before, 1, 0).astype(jnp.int32)
    numbers = lax.broadcasted_iota(jnp.int32, (1, capacity, 1), 1)
    place = mask[:, None, :] & (slots[:, None, :] == numbers)
    g_buf = jnp.sum(jnp.where(place, weight[:, None, :], 0.0), axis=2).astype(BF16)

    def dispatch(source, member):
        chosen = place[:, member * part:(member + 1) * part].astype(BF16).reshape(-1, tok_count)
        pieces = [
            dot(chosen, source[:, p * width:(p + 1) * width], 1, 0).astype(BF16)
            for p in range(count_dp)
        ]
        buffer = jnp.stack(pieces).reshape(blocks, part, width)
        got = lax.all_to_all(buffer, BLOCKS, split_axis=0, concat_axis=0, tiled=True)
        return got.reshape(rows, width)

    arrived = []
    for member in range(PARTS):
        arrived.append((dispatch(tokens, member), dispatch(cotangent, member)))
    g_send = jnp.broadcast_to(g_buf[None], (count_dp, experts, capacity)).reshape(blocks, capacity)
    g_in = lax.all_to_all(g_send, BLOCKS, split_axis=0, concat_axis=0, tiled=True).astype(F32)

    w_gate_cut = w_gate.reshape(count_tensor, width // count_tensor, units)
    w_up_cut = w_up.reshape(count_tensor, width // count_tensor, units)
    kept, gate_parts, returned = [], [], []
    for member in range(PARTS):
        x_rows, dy_rows = arrived[member]
        factor = g_in[:, member * part:(member + 1) * part].reshape(rows, 1)
        gate_pre = dp_sum(dot(x_rows, w_gate, 1, 0))
        up_pre = dp_sum(dot(x_rows, w_up, 1, 0))
        back = dp_sum(dot(dy_rows, w_down, 1, 0))
        sigma = jax.nn.sigmoid(gate_pre)
        active = gate_pre * sigma
        hidden = (active * up_pre).astype(BF16)
        gate_parts.append(jnp.sum(hidden.astype(F32) * back, axis=1).reshape(blocks, part))
        hidden_grad = factor * back
        d_gate = (hidden_grad * up_pre * sigma * (1.0 + gate_pre * (1.0 - sigma))).astype(BF16)
        d_up = (hidden_grad * active).astype(BF16)
        scaled = (factor * dy_rows.astype(F32)).astype(BF16)
        kept.append((x_rows, d_gate, d_up, scaled, hidden))
        slot_input = dot(d_gate, w_gate_cut, 1, 2) + dot(d_up, w_up_cut, 1, 2)
        slot_input = jnp.swapaxes(slot_input.astype(BF16), 0, 1)
        share = lax.psum_scatter(slot_input, "tensor", scatter_dimension=0, tiled=False)
        share = share.astype(BF16).reshape(blocks, part, -1)
        returned.append(lax.all_to_all(share, BLOCKS, split_axis=0, concat_axis=0, tiled=True))

    x_all, d_gate, d_up, scaled, hidden = [jnp.concatenate(group, 0) for group in zip(*kept)]
    grad_gate = dot(x_all, d_gate, 0, 0).astype(BF16)
    grad_up = dot(x_all, d_up, 0, 0).astype(BF16)
    grad_down = dot(scaled, hidden, 0, 0).astype(BF16)

    slot_gate = jnp.concatenate(gate_parts, 1).astype(BF16)
    everyone = lax.all_gather(slot_gate, ("expert", "tensor"), axis=0, tiled=False)
    mine = lax.axis_index("dp") * experts + lax.axis_index("expert")
    own = lax.dynamic_index_in_dim(everyone, mine, 1, keepdims=False)
    own = jnp.sum(own.reshape(experts, count_tensor, capacity).astype(F32), axis=1)
    own = own.astype(BF16).astype(F32)
    at_token = jnp.sum(jnp.where(place, own[:, :, None], 0.0), axis=1)
    gate_grad = jnp.sum(jnp.where(named, at_token[:, :, None], 0.0), axis=0).astype(BF16)

    chunk = width // count_tensor
    joined = jnp.concatenate(
        [r.reshape(count_dp, experts, part, chunk) for r in returned], axis=2
    ).reshape(count_dp, experts * capacity, chunk)
    chosen = place.astype(BF16).reshape(experts * capacity, tok_count)
    picked = jnp.stack([dot(chosen, joined[p], 0, 0).astype(BF16) for p in range(count_dp)])
    whole = lax.all_gather(picked, "tensor", axis=0, tiled=False)
    input_grad = jnp.transpose(whole, (2, 1, 0, 3)).reshape(tok_count, model_width)
    return (input_grad, gate_grad, grad_gate[None], grad_up[None], grad_down[None])


def solution(mesh):
    tokens = P(("dp", "expert"), None)
    weights = P("expert", "dp", "tensor")
    return jax.shard_map(
        on_device,
        mesh=mesh,
        in_specs=(tokens, tokens, tokens, tokens, weights, weights, weights),
        out_specs=(tokens, tokens, weights, weights, weights),
        check_vma=False,
    )
```

```python
import jax
import jax.numpy as jnp
from jax import lax
from jax.sharding import PartitionSpec as P

F32, BF16 = jnp.float32, jnp.bfloat16
PARTS = 2
BLOCKS = ("dp", "expert")
FEW = 8


def dot(left, right, left_dim, right_dim):
    return lax.dot_general(
        left, right, (((left_dim,), (right_dim,)), ((), ())), preferred_element_type=F32
    )


def dp_sum(partial):
    count = lax.axis_size("dp")
    sent = partial.astype(BF16)
    total = partial
    for shift in range(1, count):
        moved = lax.ppermute(sent, "dp", [(i, (i + shift) % count) for i in range(count)])
        total = total + moved.astype(F32)
    return total


def block_shift(value, shift_dp, shift_expert, back=False):
    count_dp, experts = lax.axis_size("dp"), lax.axis_size("expert")
    pairs = []
    for p in range(count_dp):
        for q in range(experts):
            there = (p + shift_dp) % count_dp * experts + (q + shift_expert) % experts
            here = p * experts + q
            pairs.append((there, here) if back else (here, there))
    return lax.ppermute(value, BLOCKS, pairs)


def tensor_shift(value, shift):
    count = lax.axis_size("tensor")
    return lax.ppermute(value, "tensor", [(i, (i + shift) % count) for i in range(count)])


def after(value, *earlier):
    return lax.optimization_barrier((value,) + earlier)[0]


def tensor_scatter(cut):
    count = lax.axis_size("tensor")
    if count > FEW:
        return lax.psum_scatter(cut, "tensor", scatter_dimension=0, tiled=False).astype(BF16)
    me = lax.axis_index("tensor")
    total = lax.dynamic_index_in_dim(cut, me, 0, keepdims=False).astype(F32)
    for shift in range(1, count):
        piece = lax.dynamic_index_in_dim(cut, (me + shift) % count, 0, keepdims=False)
        total = total + tensor_shift(piece, shift).astype(F32)
    return total.astype(BF16)


def tensor_total(value):
    count = lax.axis_size("tensor")
    if count > FEW:
        return lax.psum(value, "tensor").astype(BF16)
    total = value.astype(F32)
    for shift in range(1, count):
        total = total + tensor_shift(value, shift).astype(F32)
    return total.astype(BF16)


def tensor_gather(value):
    count = lax.axis_size("tensor")
    if count > FEW:
        return lax.all_gather(value, "tensor", axis=0, tiled=False)
    me = lax.axis_index("tensor")
    onward = [value] + [tensor_shift(value, shift) for shift in range(count - 1, 0, -1)]
    twice = jnp.stack(onward + onward)
    return lax.dynamic_slice_in_dim(twice, (count - me) % count, count, 0)


def on_device(tokens, cotangent, gate_weights, expert_ids, w_gate, w_up, w_down):
    experts = lax.axis_size("expert")
    count_dp = lax.axis_size("dp")
    count_tensor = lax.axis_size("tensor")
    my_dp, my_expert = lax.axis_index("dp"), lax.axis_index("expert")
    blocks = count_dp * experts
    tok_count, model_width = tokens.shape
    capacity = tok_count * 3 // experts
    part = capacity // PARTS
    w_gate, w_up, w_down = w_gate[0], w_up[0], w_down[0]
    width, units = w_gate.shape
    rows = blocks * part
    steps = [(i, j) for i in range(count_dp) for j in range(experts)]

    labels = (lax.broadcasted_iota(jnp.int32, (experts, 1, 1), 0) + my_expert) % experts
    named = expert_ids[None] == labels
    mask = jnp.any(named, axis=2)
    weight = jnp.sum(jnp.where(named, gate_weights[None].astype(F32), 0.0), axis=2)
    earlier_row = lax.broadcasted_iota(jnp.int32, (tok_count, tok_count), 0)
    earlier_col = lax.broadcasted_iota(jnp.int32, (tok_count, tok_count), 1)
    before = (earlier_row < earlier_col).astype(BF16)
    slots = dot(mask.astype(BF16), before, 1, 0).astype(jnp.int32)
    numbers = lax.broadcasted_iota(jnp.int32, (1, capacity, 1), 1)
    place = mask[:, None, :] & (slots[:, None, :] == numbers)
    g_buf = jnp.sum(jnp.where(place, weight[:, None, :], 0.0), axis=2).astype(BF16)

    def halves(source):
        return [
            lax.dynamic_slice_in_dim(source, (my_dp + i) % count_dp * width, width, 1)
            for i in range(count_dp)
        ]

    def by_dp(pieces):
        ordered = []
        for d in range(count_dp):
            for j in range(experts):
                piece = pieces[j]
                for i in range(1, count_dp):
                    piece = jnp.where((my_dp + count_dp - i) % count_dp == d, pieces[i * experts + j], piece)
                ordered.append(piece)
        return jnp.concatenate(ordered, 0)

    def dispatch(source_halves, member):
        got = []
        for i, j in steps:
            chosen = place[j, member * part:(member + 1) * part].astype(BF16)
            piece = dot(chosen, source_halves[i], 1, 0).astype(BF16)
            got.append(block_shift(piece, i, j) if i or j else piece)
        return by_dp(got)

    def block_of(array, i, j):
        at = (my_dp + count_dp - i) % count_dp * experts + j
        return lax.dynamic_index_in_dim(array, at, 0, keepdims=False)

    token_halves, grad_halves = halves(tokens), halves(cotangent)
    arrived = [(dispatch(token_halves, 0), dispatch(grad_halves, 0))]
    g_own = jnp.stack([block_shift(g_buf[j], 0, j) if j else g_buf[0] for j in range(experts)])
    g_got = [block_shift(g_own, i, 0) if i else g_own for i in range(count_dp)]
    g_in = by_dp([g_got[i][j:j + 1] for i, j in steps]).astype(F32)
    for member in range(1, PARTS):
        x_before, dy_before = arrived[-1]
        arrived.append((
            dispatch([after(half, x_before) for half in token_halves], member),
            dispatch([after(half, dy_before) for half in grad_halves], member),
        ))

    w_gate_cut = w_gate.reshape(count_tensor, width // count_tensor, units)
    w_up_cut = w_up.reshape(count_tensor, width // count_tensor, units)
    kept, gate_parts, returned = [], [], []
    for member in range(PARTS):
        x_rows, dy_rows = arrived[member]
        if member:
            dy_rows = after(dy_rows, slot_input)
        factor = g_in[:, member * part:(member + 1) * part].reshape(rows, 1)
        gate_pre = dp_sum(dot(x_rows, w_gate, 1, 0))
        up_pre = dp_sum(dot(x_rows, w_up, 1, 0))
        back = dp_sum(dot(dy_rows, w_down, 1, 0))
        sigma = jax.nn.sigmoid(gate_pre)
        active = gate_pre * sigma
        hidden = (active * up_pre).astype(BF16)
        gate_parts.append(jnp.sum(hidden.astype(F32) * back, axis=1).reshape(blocks, part))
        hidden_grad = factor * back
        d_gate = (hidden_grad * up_pre * sigma * (1.0 + gate_pre * (1.0 - sigma))).astype(BF16)
        d_up = (hidden_grad * active).astype(BF16)
        scaled = (factor * dy_rows.astype(F32)).astype(BF16)
        kept.append((x_rows, d_gate, d_up, scaled, hidden))
        slot_input = dot(d_gate, w_gate_cut, 1, 2) + dot(d_up, w_up_cut, 1, 2)
        slot_input = jnp.swapaxes(slot_input.astype(BF16), 0, 1)
        share = tensor_scatter(slot_input).reshape(blocks, part, -1)
        returned.append([
            block_shift(block_of(share, i, j), i, j, back=True) if i or j else block_of(share, 0, 0)
            for i, j in steps
        ])

    slot_gate = tensor_total(jnp.concatenate(gate_parts, 1).astype(BF16))
    own = jnp.stack([
        block_shift(block_of(slot_gate, 0, j), 0, j, back=True) if j else block_of(slot_gate, 0, 0)
        for j in range(experts)
    ]).astype(F32)
    at_token = jnp.sum(jnp.where(place, own[:, :, None], 0.0), axis=1)
    gate_grad = jnp.sum(jnp.where(named, at_token[:, :, None], 0.0), axis=0).astype(BF16)

    kept = [jnp.concatenate(group, 0) for group in zip(*kept)]
    x_all, d_gate, d_up, scaled, hidden = kept
    x_all, scaled = after(x_all, slot_input), after(scaled, slot_input)
    grad_gate = dot(x_all, d_gate, 0, 0).astype(BF16)
    grad_up = dot(x_all, d_up, 0, 0).astype(BF16)
    grad_down = dot(scaled, hidden, 0, 0).astype(BF16)

    picked = []
    for i in range(count_dp):
        joined = jnp.concatenate(
            [returned[m][i * experts + j] for m in range(PARTS) for j in range(experts)], 0
        )
        chosen = jnp.concatenate(
            [place[:, m * part:(m + 1) * part].reshape(-1, tok_count) for m in range(PARTS)], 0
        )
        picked.append(dot(chosen.astype(BF16), joined, 0, 0).astype(BF16))
    stacked = jnp.stack(picked)
    picked = jnp.stack([
        lax.dynamic_index_in_dim(stacked, (p - my_dp + count_dp) % count_dp, 0, keepdims=False)
        for p in range(count_dp)
    ])
    whole = tensor_gather(picked)
    input_grad = jnp.transpose(whole, (2, 1, 0, 3)).reshape(tok_count, model_width)
    return (input_grad, gate_grad, grad_gate[None], grad_up[None], grad_down[None])


def solution(mesh):
    tokens = P(("dp", "expert"), None)
    weights = P("expert", "dp", "tensor")
    return jax.shard_map(
        on_device,
        mesh=mesh,
        in_specs=(tokens, tokens, tokens, tokens, weights, weights, weights),
        out_specs=(tokens, tokens, weights, weights, weights),
        check_vma=False,
    )
```

```python
import jax
import jax.numpy as jnp
from jax import lax
from jax.sharding import PartitionSpec as P

F32, BF16 = jnp.float32, jnp.bfloat16
PARTS = 2
BLOCKS = ("dp", "expert")
FEW = 8
LANES = 128


def dot(left, right, left_dim, right_dim):
    return lax.dot_general(
        left, right, (((left_dim,), (right_dim,)), ((), ())), preferred_element_type=F32
    )


def dp_sum(partial):
    count = lax.axis_size("dp")
    sent = partial.astype(BF16)
    total = partial
    for shift in range(1, count):
        moved = lax.ppermute(sent, "dp", [(i, (i + shift) % count) for i in range(count)])
        total = total + moved.astype(F32)
    return total


def block_shift(value, shift_dp, shift_expert, back=False):
    count_dp, experts = lax.axis_size("dp"), lax.axis_size("expert")
    pairs = []
    for p in range(count_dp):
        for q in range(experts):
            there = (p + shift_dp) % count_dp * experts + (q + shift_expert) % experts
            here = p * experts + q
            pairs.append((there, here) if back else (here, there))
    return lax.ppermute(value, BLOCKS, pairs)


def tensor_shift(value, shift):
    count = lax.axis_size("tensor")
    return lax.ppermute(value, "tensor", [(i, (i + shift) % count) for i in range(count)])


def after(value, *earlier):
    return lax.optimization_barrier((value,) + earlier)[0]


def tensor_scatter(cut):
    count = lax.axis_size("tensor")
    if count > FEW:
        return lax.psum_scatter(cut, "tensor", scatter_dimension=0, tiled=False).astype(BF16)
    me = lax.axis_index("tensor")
    total = lax.dynamic_index_in_dim(cut, me, 0, keepdims=False).astype(F32)
    for shift in range(1, count):
        piece = lax.dynamic_index_in_dim(cut, (me + shift) % count, 0, keepdims=False)
        total = total + tensor_shift(piece, shift).astype(F32)
    return total.astype(BF16)


def tensor_total(value):
    count = lax.axis_size("tensor")
    if count > FEW:
        return lax.psum(value, "tensor").astype(BF16)
    total = value.astype(F32)
    for shift in range(1, count):
        total = total + tensor_shift(value, shift).astype(F32)
    return total.astype(BF16)


def tensor_gather(value):
    count = lax.axis_size("tensor")
    if count > FEW:
        return lax.all_gather(value, "tensor", axis=0, tiled=False)
    me = lax.axis_index("tensor")
    onward = [value] + [tensor_shift(value, shift) for shift in range(count - 1, 0, -1)]
    twice = jnp.stack(onward + onward)
    return lax.dynamic_slice_in_dim(twice, (count - me) % count, count, 0)


def on_device(tokens, cotangent, gate_weights, expert_ids, w_gate, w_up, w_down):
    experts = lax.axis_size("expert")
    count_dp = lax.axis_size("dp")
    count_tensor = lax.axis_size("tensor")
    my_dp, my_expert = lax.axis_index("dp"), lax.axis_index("expert")
    blocks = count_dp * experts
    tok_count, model_width = tokens.shape
    capacity = tok_count * 3 // experts
    part = capacity // PARTS
    w_gate, w_up, w_down = w_gate[0], w_up[0], w_down[0]
    width, units = w_gate.shape
    steps = [(i, j) for i in range(count_dp) for j in range(experts)]

    labels = (lax.broadcasted_iota(jnp.int32, (experts, 1, 1), 0) + my_expert) % experts
    named = expert_ids[None] == labels
    mask = jnp.any(named, axis=2)
    weight = jnp.sum(jnp.where(named, gate_weights[None].astype(F32), 0.0), axis=2)
    earlier_row = lax.broadcasted_iota(jnp.int32, (tok_count, tok_count), 0)
    earlier_col = lax.broadcasted_iota(jnp.int32, (tok_count, tok_count), 1)
    before = (earlier_row < earlier_col).astype(BF16)
    slots = dot(mask.astype(BF16), before, 1, 0).astype(jnp.int32)
    numbers = lax.broadcasted_iota(jnp.int32, (1, capacity, 1), 1)
    place = mask[:, None, :] & (slots[:, None, :] == numbers)
    g_buf = jnp.sum(jnp.where(place, weight[:, None, :], 0.0), axis=2).astype(BF16)

    def halves(source):
        return [
            lax.dynamic_slice_in_dim(source, (my_dp + i) % count_dp * width, width, 1)
            for i in range(count_dp)
        ]

    def by_dp(pieces):
        ordered = []
        for d in range(count_dp):
            for j in range(experts):
                piece = pieces[j]
                for i in range(1, count_dp):
                    piece = jnp.where((my_dp + count_dp - i) % count_dp == d, pieces[i * experts + j], piece)
                ordered.append(piece)
        return jnp.concatenate(ordered, 0)

    def dispatch(source_halves, member, with_weight=False):
        got = []
        for i, j in steps:
            chosen = place[j, member * part:(member + 1) * part].astype(BF16)
            piece = dot(chosen, source_halves[i], 1, 0).astype(BF16)
            if with_weight:
                column = g_buf[j, member * part:(member + 1) * part][:, None]
                piece = jnp.concatenate([piece, jnp.broadcast_to(column, (part, LANES))], 1)
            got.append(block_shift(piece, i, j) if i or j else piece)
        return by_dp(got)

    def block_of(array, i, j):
        at = (my_dp + count_dp - i) % count_dp * experts + j
        return lax.dynamic_index_in_dim(array, at, 0, keepdims=False)

    token_halves, grad_halves = halves(tokens), halves(cotangent)
    arrived = [(dispatch(token_halves, 0), dispatch(grad_halves, 0, True))]
    for member in range(1, PARTS):
        x_before, dy_before = arrived[-1]
        arrived.append((
            dispatch([after(half, x_before) for half in token_halves], member),
            dispatch([after(half, dy_before) for half in grad_halves], member, True),
        ))

    w_gate_cut = w_gate.reshape(count_tensor, width // count_tensor, units)
    w_up_cut = w_up.reshape(count_tensor, width // count_tensor, units)
    kept, gate_parts, returned = [], [], []
    for member in range(PARTS):
        x_rows, dy_wide = arrived[member]
        dy_rows, factor = dy_wide[:, :width], dy_wide[:, width:width + 1].astype(F32)
        gate_pre = dp_sum(dot(x_rows, w_gate, 1, 0))
        up_pre = dp_sum(dot(x_rows, w_up, 1, 0))
        back = dp_sum(dot(dy_rows, w_down, 1, 0))
        sigma = jax.nn.sigmoid(gate_pre)
        active = gate_pre * sigma
        hidden = (active * up_pre).astype(BF16)
        gate_parts.append(jnp.sum(hidden.astype(F32) * back, axis=1).reshape(blocks, part))
        hidden_grad = factor * back
        d_gate = (hidden_grad * up_pre * sigma * (1.0 + gate_pre * (1.0 - sigma))).astype(BF16)
        d_up = (hidden_grad * active).astype(BF16)
        scaled = (factor * dy_rows.astype(F32)).astype(BF16)
        kept.append((x_rows, d_gate, d_up, scaled, hidden))
        slot_input = dot(d_gate, w_gate_cut, 1, 2) + dot(d_up, w_up_cut, 1, 2)
        slot_input = jnp.swapaxes(slot_input.astype(BF16), 0, 1)
        share = tensor_scatter(slot_input).reshape(blocks, part, -1)
        returned.append([
            block_shift(block_of(share, i, j), i, j, back=True) if i or j else block_of(share, 0, 0)
            for i, j in steps
        ])

    slot_gate = tensor_total(jnp.concatenate(gate_parts, 1).astype(BF16))
    own = jnp.stack([
        block_shift(block_of(slot_gate, 0, j), 0, j, back=True) if j else block_of(slot_gate, 0, 0)
        for j in range(experts)
    ]).astype(F32)
    at_token = jnp.sum(jnp.where(place, own[:, :, None], 0.0), axis=1)
    gate_grad = jnp.sum(jnp.where(named, at_token[:, :, None], 0.0), axis=0).astype(BF16)

    kept = [jnp.concatenate(group, 0) for group in zip(*kept)]
    x_all, d_gate, d_up, scaled, hidden = kept
    x_all, scaled = after(x_all, slot_input), after(scaled, slot_input)
    grad_gate = dot(x_all, d_gate, 0, 0).astype(BF16)
    grad_up = dot(x_all, d_up, 0, 0).astype(BF16)
    grad_down = dot(scaled, hidden, 0, 0).astype(BF16)

    picked = []
    for i in range(count_dp):
        joined = jnp.concatenate(
            [returned[m][i * experts + j] for m in range(PARTS) for j in range(experts)], 0
        )
        chosen = jnp.concatenate(
            [place[:, m * part:(m + 1) * part].reshape(-1, tok_count) for m in range(PARTS)], 0
        )
        picked.append(dot(chosen.astype(BF16), joined, 0, 0).astype(BF16))
    stacked = jnp.stack(picked)
    picked = jnp.stack([
        lax.dynamic_index_in_dim(stacked, (p - my_dp + count_dp) % count_dp, 0, keepdims=False)
        for p in range(count_dp)
    ])
    whole = tensor_gather(picked)
    input_grad = jnp.transpose(whole, (2, 1, 0, 3)).reshape(tok_count, model_width)
    return (input_grad, gate_grad, grad_gate[None], grad_up[None], grad_down[None])


def solution(mesh):
    tokens = P(("dp", "expert"), None)
    weights = P("expert", "dp", "tensor")
    return jax.shard_map(
        on_device,
        mesh=mesh,
        in_specs=(tokens, tokens, tokens, tokens, weights, weights, weights),
        out_specs=(tokens, tokens, weights, weights, weights),
        check_vma=False,
    )
```
